32 devices in a mesh: lat: 4 (over z), lon: 4 (over y, core), buf: 2 (over x).
Axes of the slice: x: 2, y: 2, z: 4, core: 2. Of those that a mesh axis runs over, the one named last changes fastest.
Arguments:
- store: bfloat16 [8, 64, 64, 1725], P('buf', ('lat', 'lon')), may hold values from -6 to 6
- sample_index: int32 [6], replicated, may hold values from 0 to 7, as said below
- region_ids: int32 [64, 64], replicated, may hold values from 0 to 2
- w_embed: bfloat16 [1725, 512], replicated, may hold values from -0.15625 to 0.15625
- attn_gain: float32 [512], replicated, may hold values from 0.1 to 1.9
- w_qkv: bfloat16 [512, 1536], replicated, may hold values from -8 to 8
- w_out: bfloat16 [512, 512], replicated, may hold values from -0.25 to 0.25
- out_gain: float32 [512], replicated, may hold values from 0.1 to 1.9
- w_dec: bfloat16 [512, 1725], replicated, may hold values from -0.25 to 0.25
Outputs:
- new_store: bfloat16 [8, 64, 64, 1725], P('buf', ('lat', 'lon'))
The draws below stay inside these ranges and needn't reach their ends.
Inputs may be any that keep to these rules, and one draw needn't show every extreme that they name: `sample_index`: distinct slot numbers.
All inputs are finite; a program needn't handle non-finite values.
Results may differ from the reference program's by a relative error of at most 0.007.
Values may be sent and summed in bfloat16 or wider, within the bound.
A program may use at most 128 MiB of HBM per device.

```python
import math
import jax
import jax.numpy as jnp
from jax import lax

D = 512
HEADS = 8
HDIM = 64
CPP = 1725
WIN = 8
SLOTS = 8
B = 6
HT = 64
WT = 64


def draw_sample_index(key, part):
    order = jax.random.permutation(jax.random.fold_in(key, 21), SLOTS)
    return order[:B].astype(jnp.int32)


def draw_w_qkv(key, part):
    entries = jax.random.normal(jax.random.fold_in(key, 11), (D, 3 * D), jnp.float32)
    entries = jnp.clip(entries, -6.0, 6.0) * D ** (-0.5)
    return jnp.clip(entries, -8.0, 8.0).astype(jnp.bfloat16)


def touch_ends(result, stream_key, least, top_value):
    longest = result.shape.index(max(result.shape))
    spots = []
    for shift in (0, 1):
        where = [jax.random.randint(jax.random.fold_in(stream_key, axis), (), 0, length) for axis, length in enumerate(result.shape)]
        where[longest] = (where[longest] + shift) % result.shape[longest]
        spots.append(tuple(where))
    return result.at[spots[0]].set(least).at[spots[1]].set(top_value)


def shard_levels(own_key, shape, split, low, largest):
    factor_of, own = 1.0, jax.random.fold_in(own_key, 6)
    for dim, shards_of in split:
        heights = jnp.exp(jax.random.uniform(jax.random.fold_in(own, dim), (shards_of,), jnp.float32, low / len(split), largest / len(split)))
        factor_of = factor_of * jnp.repeat(heights, shape[dim] // shards_of).reshape([-1 if axis == dim else 1 for axis in range(len(shape))])
    return factor_of


def gaussian(stream_key, dims, width, most, cuts=(), kind=jnp.bfloat16):
    array = jax.random.normal(stream_key, dims, jnp.float32) * width
    if len(cuts) > 0:
        array = shard_levels(stream_key, dims, cuts, -0.22, 0.18) * array
    return jnp.clip(array, min=-most, max=most).astype(kind)


def setup_inputs(seed: int = 0) -> dict:
    streams_of = jax.random.split(jax.random.key(seed), 10)
    store = gaussian(streams_of[0], (SLOTS, HT, WT, CPP), 1.0, 6.0, ((0, 2), (1, 16)))
    sample_index = draw_sample_index(jax.random.fold_in(streams_of[9], 71), 0)
    region_ids = touch_ends(jax.random.randint(streams_of[2], (HT, WT), 0, 3), jax.random.fold_in(streams_of[2], 1), 0, 2).astype(jnp.int32)
    w_embed = gaussian(streams_of[3], (CPP, D), CPP ** -0.5, 0.15625)
    attn_gain = jnp.clip(1.0 + 0.18 * jax.random.normal(streams_of[4], (D,), jnp.float32), 0.1, 1.9)
    w_qkv = draw_w_qkv(jax.random.fold_in(streams_of[9], 71), 0)
    w_out = gaussian(streams_of[6], (D, D), D ** -0.5, 0.25)
    out_gain = jnp.clip(1.0 + 0.18 * jax.random.normal(streams_of[7], (D,), jnp.float32), 0.1, 1.9)
    w_dec = gaussian(streams_of[8], (D, CPP), D ** -0.5, 0.25)
    return dict(store=store, sample_index=sample_index, region_ids=region_ids, w_embed=w_embed, attn_gain=attn_gain, w_qkv=w_qkv, w_out=w_out, out_gain=out_gain, w_dec=w_dec)


def layer_norm(values, gain_row):
    center = lax.optimization_barrier(jnp.mean(values, axis=-1, keepdims=True))
    spread = lax.optimization_barrier(jnp.mean(jnp.square(values - center), axis=-1, keepdims=True))
    return (values - center) * lax.rsqrt(spread + 1e-05) * gain_row

def window_attention(windows, regions):
    queries = windows[:, :, 0].astype(jnp.float32)
    keys_all = windows[:, :, 1].astype(jnp.float32)
    values_all = windows[:, :, 2].astype(jnp.float32)
    scores = jnp.einsum('wqhd,wkhd->whqk', queries, keys_all) / math.sqrt(HDIM)
    visible = (regions[:, :, None] == regions[:, None, :])[:, None]
    scores = jnp.where(visible, scores, -1e+30)
    highest = lax.optimization_barrier(jnp.max(scores, axis=-1, keepdims=True))
    expo_terms = jnp.where(visible, jnp.exp(scores - highest), 0.0)
    weights = (expo_terms / lax.optimization_barrier(jnp.sum(expo_terms, axis=-1, keepdims=True))).astype(jnp.bfloat16)
    mixed_heads = jnp.einsum('whqk,wkhd->wqhd', weights.astype(jnp.float32), values_all)
    return mixed_heads.astype(jnp.bfloat16).reshape(windows.shape[0], WIN * WIN, D)

def reference(store, sample_index, region_ids, w_embed, attn_gain, w_qkv, w_out, out_gain, w_dec):
    half_win = WIN // 2
    rolled_regions = jnp.roll(region_ids, (-half_win, -half_win), axis=(0, 1))
    region_windows = rolled_regions.reshape(HT // WIN, WIN, WT // WIN, WIN).transpose(0, 2, 1, 3).reshape(-1, WIN * WIN)

    def one_sample(slot_number):
        state_grid = lax.dynamic_index_in_dim(store, slot_number, 0, keepdims=False)
        patches = state_grid.reshape(HT * WT, CPP)
        embedded = jnp.dot(patches, w_embed, preferred_element_type=jnp.float32).astype(jnp.bfloat16)
        normed = layer_norm(embedded.astype(jnp.float32), attn_gain).astype(jnp.bfloat16)
        projected = jnp.dot(normed, w_qkv, preferred_element_type=jnp.float32).astype(jnp.bfloat16)
        rolled = jnp.roll(projected.reshape(HT, WT, 3 * D), (-half_win, -half_win), axis=(0, 1))
        windows = rolled.reshape(HT // WIN, WIN, WT // WIN, WIN, 3, HEADS, HDIM)
        windows = windows.transpose(0, 2, 1, 3, 4, 5, 6).reshape(-1, WIN * WIN, 3, HEADS, HDIM)
        mixed_heads = window_attention(windows, region_windows)
        placed = mixed_heads.reshape(HT // WIN, WT // WIN, WIN, WIN, D).transpose(0, 2, 1, 3, 4).reshape(HT, WT, D)
        placed = jnp.roll(placed, (half_win, half_win), axis=(0, 1)).reshape(HT * WT, D)
        updated = embedded.astype(jnp.float32) + jnp.dot(placed, w_out, preferred_element_type=jnp.float32)
        final_norm = layer_norm(updated, out_gain).astype(jnp.bfloat16)
        predicted = (patches.astype(jnp.float32) + jnp.dot(final_norm, w_dec, preferred_element_type=jnp.float32)).astype(jnp.bfloat16)
        return predicted.reshape(HT, WT, CPP)
    predictions = lax.map(one_sample, sample_index)
    return store.at[sample_index].set(predictions)
```

```python
import functools
import math

import jax
import jax.numpy as jnp
from jax import lax
from jax.experimental import pallas as pl
from jax.experimental.pallas import tpu as pltpu
from jax.sharding import PartitionSpec as P

D = 512
HEADS = 8
HDIM = 64
WIN = 8
HALF = WIN // 2
VMEM_LIMIT = 56 * 1024 * 1024


def with_halo(array, sides, width):
    for axis, dim in sides:
        devices, length = (lax.axis_size(axis), array.shape[dim])
        up = [(i, (i + 1) % devices) for i in range(devices)]
        down = [(j, i) for i, j in up]
        last = lax.slice_in_dim(array, length - width, length, axis=dim)
        leading = lax.slice_in_dim(array, 0, width, axis=dim)
        before = lax.ppermute(last, axis, up)
        after = lax.ppermute(leading, axis, down)
        array = jnp.concatenate([before, array, after], axis=dim)
    return array


def layer_norm(values, gain_row):
    center = jnp.mean(values, axis=-1, keepdims=True)
    spread = jnp.mean(jnp.square(values - center), axis=-1, keepdims=True)
    return (values - center) * lax.rsqrt(spread + 1e-05) * gain_row


def window_mix(windows, regions):
    scores = jnp.einsum(
        "bwqhd,bwkhd->bwhqk",
        windows[:, :, :, 0],
        windows[:, :, :, 1],
        preferred_element_type=jnp.float32,
    ) / math.sqrt(HDIM)
    visible = (regions[:, :, None] == regions[:, None, :])[None, :, None]
    scores = jnp.where(visible, scores, -1e30)
    highest = jnp.max(scores, axis=-1, keepdims=True)
    expo_terms = jnp.where(visible, jnp.exp(scores - highest), 0.0)
    weights = (expo_terms / jnp.sum(expo_terms, axis=-1, keepdims=True)).astype(jnp.bfloat16)
    return jnp.einsum(
        "bwhqk,bwkhd->bwqhd", weights, windows[:, :, :, 2], preferred_element_type=jnp.float32
    ).astype(jnp.bfloat16)


def local_tiles(store, sample_index, region_ids, w_embed, attn_gain, w_qkv, w_out, out_gain, w_dec):
    lon_count = lax.axis_size("lon")
    slots_here, rows_here, width_all, patch_len = store.shape
    patch_cols = width_all // lon_count
    patch_rows = rows_here * lon_count
    half_win = WIN // 2
    ext_rows = patch_rows + WIN
    ext_cols = patch_cols + WIN
    own_slots = lax.axis_index("buf") * slots_here + jnp.arange(slots_here, dtype=jnp.int32)
    matches = own_slots[:, None] == sample_index[None, :]
    occupied = jnp.any(matches, axis=1)
    local_rows = store.reshape(slots_here, 1, rows_here, lon_count, patch_cols, patch_len)
    tile_data = lax.all_to_all(local_rows, "lon", split_axis=3, concat_axis=1, tiled=True)
    patches = tile_data.reshape(-1, patch_len)
    embedded = jnp.dot(patches, w_embed, preferred_element_type=jnp.float32).astype(jnp.bfloat16)
    normed = layer_norm(embedded.astype(jnp.float32), attn_gain).astype(jnp.bfloat16)
    normed = normed.reshape(slots_here, patch_rows, patch_cols, D)
    widened = with_halo(normed, (("lat", 1), ("lon", 2)), half_win)
    projected = jnp.dot(widened.reshape(-1, D), w_qkv, preferred_element_type=jnp.float32).astype(
        jnp.bfloat16
    )
    windows = projected.reshape(
        slots_here, ext_rows // WIN, WIN, ext_cols // WIN, WIN, 3, HEADS, HDIM
    )
    windows = windows.transpose(0, 1, 3, 2, 4, 5, 6, 7).reshape(
        slots_here, -1, WIN * WIN, 3, HEADS, HDIM
    )
    total_rows, total_cols = region_ids.shape
    row_pick = (
        lax.axis_index("lat") * patch_rows - half_win + jnp.arange(ext_rows, dtype=jnp.int32)
    ) % total_rows
    col_pick = (
        lax.axis_index("lon") * patch_cols - half_win + jnp.arange(ext_cols, dtype=jnp.int32)
    ) % total_cols
    local_regions = jnp.take(jnp.take(region_ids, row_pick, axis=0), col_pick, axis=1)
    region_windows = (
        local_regions.reshape(ext_rows // WIN, WIN, ext_cols // WIN, WIN)
        .transpose(0, 2, 1, 3)
        .reshape(-1, WIN * WIN)
    )
    mixed_heads = window_mix(windows, region_windows)
    placed = mixed_heads.reshape(slots_here, ext_rows // WIN, ext_cols // WIN, WIN, WIN, D)
    placed = placed.transpose(0, 1, 3, 2, 4, 5).reshape(slots_here, ext_rows, ext_cols, D)
    placed = placed[:, half_win : half_win + patch_rows, half_win : half_win + patch_cols].reshape(
        -1, D
    )
    updated = embedded.astype(jnp.float32) + jnp.dot(
        placed, w_out, preferred_element_type=jnp.float32
    )
    final_norm = layer_norm(updated, out_gain).astype(jnp.bfloat16)
    predicted = (
        patches.astype(jnp.float32) + jnp.dot(final_norm, w_dec, preferred_element_type=jnp.float32)
    ).astype(jnp.bfloat16)
    outgoing = predicted.reshape(slots_here, lon_count, rows_here, 1, patch_cols, patch_len)
    returned = lax.all_to_all(outgoing, "lon", split_axis=1, concat_axis=3, tiled=True)
    strip_data = returned.reshape(slots_here, rows_here, width_all, patch_len)
    return jnp.where(occupied[:, None, None, None], strip_data, store)


def to_windows(values):
    rows, cols = HALF, values.shape[0] // HALF
    parts = [pltpu.roll(values[cols * i : cols * (i + 1)], cols - HALF, 0) for i in range(rows)]
    return jnp.concatenate(
        [parts[i][WIN * c : WIN * (c + 1)] for c in range(cols // WIN) for i in range(rows)], axis=0
    )


def from_windows(values):
    rows, cols = HALF, values.shape[0] // HALF
    parts = []
    for i in range(rows):
        line = jnp.concatenate(
            [
                values[WIN * (rows * c + i) : WIN * (rows * c + i + 1)]
                for c in range(cols // WIN)
            ],
            axis=0,
        )
        parts.append(pltpu.roll(line, HALF, 0))
    return jnp.concatenate(parts, axis=0)


def embed_slot(patches, w_embed, gain):
    embedded = jnp.dot(patches, w_embed, preferred_element_type=jnp.float32).astype(jnp.bfloat16)
    embedded = to_windows(embedded.astype(jnp.float32))
    normed = layer_norm(embedded, gain).astype(jnp.bfloat16)
    return embedded.astype(jnp.bfloat16), normed


def window_scores_mix(query, keys, values, seen, head_mask, pick_mask):
    queries = jnp.concatenate([query] * HEADS, axis=0) * head_mask
    scores = lax.dot_general(
        keys, queries, (((1,), (1,)), ((), ())), preferred_element_type=jnp.float32
    )
    scores = jnp.where(seen, scores, -1e30)
    expo = jnp.exp(scores - jnp.max(scores, axis=0, keepdims=True))
    weights = (expo * (1.0 / jnp.sum(expo, axis=0, keepdims=True))).astype(jnp.bfloat16)
    tokens = query.shape[0]
    groups = []
    width = 4 * HDIM
    for g in range(HEADS // 4):
        heads = lax.dot_general(
            weights[:, 4 * tokens * g : 4 * tokens * (g + 1)],
            values[:, width * g : width * (g + 1)],
            (((0,), (0,)), ((), ())),
            preferred_element_type=jnp.float32,
        )
        heads = jnp.where(pick_mask, heads, 0.0)
        total = heads[:tokens]
        for h in range(1, 4):
            total = total + heads[tokens * h : tokens * (h + 1)]
        groups.append(total)
    return jnp.concatenate(groups, axis=1).astype(jnp.bfloat16)


def mix_slot(own, other, q_regions, k_regions, w_qkv):
    tokens = own.shape[0]
    per = WIN * HALF
    query = jnp.dot(own, w_qkv[:, :D], preferred_element_type=jnp.float32)
    query = (query * (1.0 / math.sqrt(HDIM))).astype(jnp.bfloat16)
    w_kv = w_qkv[:, D:]
    kv_own = jnp.dot(own, w_kv, preferred_element_type=jnp.float32).astype(jnp.bfloat16)
    kv_other = jnp.dot(other, w_kv, preferred_element_type=jnp.float32).astype(jnp.bfloat16)
    shape = (HEADS * per, D)
    head_mask = (
        lax.broadcasted_iota(jnp.int32, shape, 0) // per
        == lax.broadcasted_iota(jnp.int32, shape, 1) // HDIM
    )
    head_mask = jnp.where(head_mask, 1.0, 0.0).astype(jnp.bfloat16)
    shape = (4 * per, 4 * HDIM)
    pick_mask = (
        lax.broadcasted_iota(jnp.int32, shape, 0) // per
        == lax.broadcasted_iota(jnp.int32, shape, 1) // HDIM
    )
    mixed = []
    for c in range(tokens // per):
        at = slice(per * c, per * (c + 1))
        kv = jnp.concatenate([kv_own[at], kv_other[at]], axis=0)
        seen = k_regions[c] == q_regions[c]
        mixed.append(
            window_scores_mix(query[at], kv[:, :D], kv[:, D:], seen, head_mask, pick_mask)
        )
    return jnp.concatenate(mixed, axis=0)


def finish_slot(embedded, mixed, w_out, gain):
    updated = embedded.astype(jnp.float32) + jnp.dot(
        mixed, w_out, preferred_element_type=jnp.float32
    )
    return from_windows(layer_norm(updated, gain)).astype(jnp.bfloat16)


def decode_slot(patches, final, w_dec_t):
    return (
        patches.astype(jnp.float32)
        + lax.dot_general(
            final, w_dec_t, (((1,), (1,)), ((), ())), preferred_element_type=jnp.float32
        )
    ).astype(jnp.bfloat16)


def embed_kernel(store_ref, w_embed_ref, gain_ref, embedded_ref, normed_ref):
    patches = store_ref[0].reshape(-1, store_ref.shape[-1])
    embedded_ref[0], normed_ref[0] = embed_slot(patches, w_embed_ref[...], gain_ref[...])


def rest_kernel(
    occupied_ref,
    store_ref,
    embedded_ref,
    own_ref,
    other_ref,
    qreg_ref,
    kreg_ref,
    w_qkv_ref,
    w_out_ref,
    gain_ref,
    w_dec_ref,
    new_ref,
):
    s = pl.program_id(0)

    @pl.when(occupied_ref[s] == 0)
    def _():
        new_ref[...] = store_ref[...]

    @pl.when(occupied_ref[s] != 0)
    def _():
        mixed = mix_slot(own_ref[0], other_ref[0], qreg_ref[...], kreg_ref[...], w_qkv_ref[...])
        final = finish_slot(embedded_ref[0], mixed, w_out_ref[...], gain_ref[...])
        patches = store_ref[0].reshape(-1, store_ref.shape[-1])
        new_ref[0] = decode_slot(patches, final, w_dec_ref[...]).reshape(store_ref.shape[1:])


def region_columns(region_ids, rows_here, mine, other):
    total_rows, cols = region_ids.shape
    rolled = jnp.roll(region_ids, -HALF, axis=1)
    strips = rolled.reshape(total_rows // rows_here, rows_here, cols // WIN, WIN)
    strips = strips.transpose(0, 2, 1, 3).reshape(total_rows // rows_here, cols // WIN, -1)
    own = lax.dynamic_index_in_dim(strips, mine, 0, keepdims=False)
    far = lax.dynamic_index_in_dim(strips, other, 0, keepdims=False)
    q_regions = jnp.tile(own, (1, HEADS))[:, None, :]
    k_regions = jnp.concatenate([own, far], axis=1)[:, :, None]
    return q_regions, k_regions


def local_strips(store, sample_index, region_ids, w_embed, attn_gain, w_qkv, w_out, out_gain, w_dec):
    slots, rows_here, cols, patch_len = store.shape
    tokens = rows_here * cols
    strips = lax.axis_size("lat") * lax.axis_size("lon")
    mine = lax.axis_index("lat") * lax.axis_size("lon") + lax.axis_index("lon")
    other = (mine + 2 * (mine % 2) - 1 + strips) % strips
    own_slots = lax.axis_index("buf") * slots + jnp.arange(slots, dtype=jnp.int32)
    occupied = jnp.any(own_slots[:, None] == sample_index[None, :], axis=1).astype(jnp.int32)
    q_regions, k_regions = region_columns(region_ids, rows_here, mine, other)
    whole = lambda shape: pl.BlockSpec(shape, lambda s, *_: (0,) * len(shape))
    slot = lambda *shape: pl.BlockSpec((1,) + shape, lambda s, *_: (s,) + (0,) * len(shape))
    params = pltpu.CompilerParams(vmem_limit_bytes=VMEM_LIMIT)
    token_shape = jax.ShapeDtypeStruct((slots, tokens, D), jnp.bfloat16)
    embedded, normed = pl.pallas_call(
        embed_kernel,
        grid=(slots,),
        in_specs=[slot(rows_here, cols, patch_len), whole(w_embed.shape), whole((1, D))],
        out_specs=[slot(tokens, D)] * 2,
        out_shape=[token_shape] * 2,
        compiler_params=params,
    )(store, w_embed, attn_gain[None])
    pairs = [(i, (i + 2 * (i % 2) - 1) % strips) for i in range(strips)]
    arrived = lax.ppermute(normed, ("lat", "lon"), pairs)
    return pl.pallas_call(
        rest_kernel,
        grid_spec=pltpu.PrefetchScalarGridSpec(
            num_scalar_prefetch=1,
            grid=(slots,),
            in_specs=[
                slot(rows_here, cols, patch_len),
                slot(tokens, D),
                slot(tokens, D),
                slot(tokens, D),
                whole(q_regions.shape),
                whole(k_regions.shape),
                whole(w_qkv.shape),
                whole(w_out.shape),
                whole((1, D)),
                whole(w_dec.shape[::-1]),
            ],
            out_specs=slot(rows_here, cols, patch_len),
        ),
        out_shape=jax.ShapeDtypeStruct(store.shape, store.dtype),
        compiler_params=params,
    )(
        occupied,
        store,
        embedded,
        normed,
        arrived,
        q_regions,
        k_regions,
        w_qkv,
        w_out,
        out_gain[None],
        w_dec.T,
    )


def local(store, *rest):
    return (local_strips if store.shape[1] == HALF else local_tiles)(store, *rest)


def solution(mesh):
    return jax.shard_map(
        local,
        mesh=mesh,
        in_specs=(P("buf", ("lat", "lon"), None, None), P(), P(), P(), P(), P(), P(), P(), P()),
        out_specs=P("buf", ("lat", "lon"), None, None),
        check_vma=False,
    )
```

```python
import functools
import math

import jax
import jax.numpy as jnp
from jax import lax
from jax.experimental import pallas as pl
from jax.experimental.pallas import tpu as pltpu
from jax.sharding import PartitionSpec as P

D = 512
HEADS = 8
HDIM = 64
WIN = 8
HALF = WIN // 2
VMEM_LIMIT = 56 * 1024 * 1024


def with_halo(array, sides, width):
    for axis, dim in sides:
        devices, length = (lax.axis_size(axis), array.shape[dim])
        up = [(i, (i + 1) % devices) for i in range(devices)]
        down = [(j, i) for i, j in up]
        last = lax.slice_in_dim(array, length - width, length, axis=dim)
        leading = lax.slice_in_dim(array, 0, width, axis=dim)
        before = lax.ppermute(last, axis, up)
        after = lax.ppermute(leading, axis, down)
        array = jnp.concatenate([before, array, after], axis=dim)
    return array


def layer_norm(values, gain_row):
    center = jnp.mean(values, axis=-1, keepdims=True)
    spread = jnp.mean(jnp.square(values - center), axis=-1, keepdims=True)
    return (values - center) * lax.rsqrt(spread + 1e-05) * gain_row


def window_mix(windows, regions):
    scores = jnp.einsum(
        "bwqhd,bwkhd->bwhqk",
        windows[:, :, :, 0],
        windows[:, :, :, 1],
        preferred_element_type=jnp.float32,
    ) / math.sqrt(HDIM)
    visible = (regions[:, :, None] == regions[:, None, :])[None, :, None]
    scores = jnp.where(visible, scores, -1e30)
    highest = jnp.max(scores, axis=-1, keepdims=True)
    expo_terms = jnp.where(visible, jnp.exp(scores - highest), 0.0)
    weights = (expo_terms / jnp.sum(expo_terms, axis=-1, keepdims=True)).astype(jnp.bfloat16)
    return jnp.einsum(
        "bwhqk,bwkhd->bwqhd", weights, windows[:, :, :, 2], preferred_element_type=jnp.float32
    ).astype(jnp.bfloat16)


def local_tiles(store, sample_index, region_ids, w_embed, attn_gain, w_qkv, w_out, out_gain, w_dec):
    lon_count = lax.axis_size("lon")
    slots_here, rows_here, width_all, patch_len = store.shape
    patch_cols = width_all // lon_count
    patch_rows = rows_here * lon_count
    half_win = WIN // 2
    ext_rows = patch_rows + WIN
    ext_cols = patch_cols + WIN
    own_slots = lax.axis_index("buf") * slots_here + jnp.arange(slots_here, dtype=jnp.int32)
    matches = own_slots[:, None] == sample_index[None, :]
    occupied = jnp.any(matches, axis=1)
    local_rows = store.reshape(slots_here, 1, rows_here, lon_count, patch_cols, patch_len)
    tile_data = lax.all_to_all(local_rows, "lon", split_axis=3, concat_axis=1, tiled=True)
    patches = tile_data.reshape(-1, patch_len)
    embedded = jnp.dot(patches, w_embed, preferred_element_type=jnp.float32).astype(jnp.bfloat16)
    normed = layer_norm(embedded.astype(jnp.float32), attn_gain).astype(jnp.bfloat16)
    normed = normed.reshape(slots_here, patch_rows, patch_cols, D)
    widened = with_halo(normed, (("lat", 1), ("lon", 2)), half_win)
    projected = jnp.dot(widened.reshape(-1, D), w_qkv, preferred_element_type=jnp.float32).astype(
        jnp.bfloat16
    )
    windows = projected.reshape(
        slots_here, ext_rows // WIN, WIN, ext_cols // WIN, WIN, 3, HEADS, HDIM
    )
    windows = windows.transpose(0, 1, 3, 2, 4, 5, 6, 7).reshape(
        slots_here, -1, WIN * WIN, 3, HEADS, HDIM
    )
    total_rows, total_cols = region_ids.shape
    row_pick = (
        lax.axis_index("lat") * patch_rows - half_win + jnp.arange(ext_rows, dtype=jnp.int32)
    ) % total_rows
    col_pick = (
        lax.axis_index("lon") * patch_cols - half_win + jnp.arange(ext_cols, dtype=jnp.int32)
    ) % total_cols
    local_regions = jnp.take(jnp.take(region_ids, row_pick, axis=0), col_pick, axis=1)
    region_windows = (
        local_regions.reshape(ext_rows // WIN, WIN, ext_cols // WIN, WIN)
        .transpose(0, 2, 1, 3)
        .reshape(-1, WIN * WIN)
    )
    mixed_heads = window_mix(windows, region_windows)
    placed = mixed_heads.reshape(slots_here, ext_rows // WIN, ext_cols // WIN, WIN, WIN, D)
    placed = placed.transpose(0, 1, 3, 2, 4, 5).reshape(slots_here, ext_rows, ext_cols, D)
    placed = placed[:, half_win : half_win + patch_rows, half_win : half_win + patch_cols].reshape(
        -1, D
    )
    updated = embedded.astype(jnp.float32) + jnp.dot(
        placed, w_out, preferred_element_type=jnp.float32
    )
    final_norm = layer_norm(updated, out_gain).astype(jnp.bfloat16)
    predicted = (
        patches.astype(jnp.float32) + jnp.dot(final_norm, w_dec, preferred_element_type=jnp.float32)
    ).astype(jnp.bfloat16)
    outgoing = predicted.reshape(slots_here, lon_count, rows_here, 1, patch_cols, patch_len)
    returned = lax.all_to_all(outgoing, "lon", split_axis=1, concat_axis=3, tiled=True)
    strip_data = returned.reshape(slots_here, rows_here, width_all, patch_len)
    return jnp.where(occupied[:, None, None, None], strip_data, store)


def to_windows(values):
    rows, cols = HALF, values.shape[0] // HALF
    parts = [pltpu.roll(values[cols * i : cols * (i + 1)], cols - HALF, 0) for i in range(rows)]
    return jnp.concatenate(
        [parts[i][WIN * c : WIN * (c + 1)] for c in range(cols // WIN) for i in range(rows)], axis=0
    )


def from_windows(values):
    rows, cols = HALF, values.shape[0] // HALF
    parts = []
    for i in range(rows):
        line = jnp.concatenate(
            [
                values[WIN * (rows * c + i) : WIN * (rows * c + i + 1)]
                for c in range(cols // WIN)
            ],
            axis=0,
        )
        parts.append(pltpu.roll(line, HALF, 0))
    return jnp.concatenate(parts, axis=0)


def embed_slot(patches, w_embed, gain):
    embedded = jnp.dot(patches, w_embed, preferred_element_type=jnp.float32).astype(jnp.bfloat16)
    embedded = to_windows(embedded.astype(jnp.float32))
    normed = layer_norm(embedded, gain).astype(jnp.bfloat16)
    return embedded.astype(jnp.bfloat16), normed


NT = (((1,), (1,)), ((), ()))
TN = (((0,), (0,)), ((), ()))
GROUP = 4
WIDE = GROUP * HDIM
PER = WIN * HALF


def attend_slot(query, kv_own, kv_other, q_regions, k_regions):
    shape = (GROUP * PER, WIDE)
    pick = (
        lax.broadcasted_iota(jnp.int32, shape, 0) // PER
        == lax.broadcasted_iota(jnp.int32, shape, 1) // HDIM
    )
    head_mask = jnp.where(pick, 1.0, 0.0).astype(jnp.bfloat16)
    windows = query.shape[0] // PER
    kvs, scores, weights, mixed = [], [], [], []
    for c in range(windows):
        at = slice(PER * c, PER * (c + 1))
        kvs.append(jnp.concatenate([kv_own[at], kv_other[at]], axis=0))
        for g in range(HEADS // GROUP):
            cols = slice(WIDE * g, WIDE * (g + 1))
            queries = jnp.concatenate([query[at, cols]] * GROUP, axis=0) * head_mask
            scores.append(
                lax.dot_general(kvs[c][:, cols], queries, NT, preferred_element_type=jnp.float32)
            )
    for c in range(windows):
        seen = k_regions[:, c : c + 1] == q_regions[c : c + 1, :]
        for g in range(HEADS // GROUP):
            part = jnp.where(seen, scores[2 * c + g], -1e30)
            expo = jnp.exp(part - jnp.max(part, axis=0, keepdims=True))
            total = jnp.sum(expo, axis=0, keepdims=True)
            weights.append((expo * (1.0 / total)).astype(jnp.bfloat16))
    for c in range(windows):
        groups = []
        for g in range(HEADS // GROUP):
            heads = lax.dot_general(
                weights[2 * c + g],
                kvs[c][:, D + WIDE * g : D + WIDE * (g + 1)],
                TN,
                preferred_element_type=jnp.float32,
            )
            heads = jnp.where(pick, heads, 0.0)
            total = heads[:PER]
            for h in range(1, GROUP):
                total = total + heads[PER * h : PER * (h + 1)]
            groups.append(total)
        mixed.append(jnp.concatenate(groups, axis=1).astype(jnp.bfloat16))
    return jnp.concatenate(mixed, axis=0)


def region_tables(own, far):
    rows, cols = own.shape
    windows = cols // WIN
    lines = [own[i : i + 1] for i in range(rows)] + [far[i : i + 1] for i in range(rows)]
    wide = jnp.concatenate([jnp.broadcast_to(line, (WIN, cols)) for line in lines], axis=0)
    row = lax.broadcasted_iota(jnp.int32, wide.shape, 0)
    col = lax.broadcasted_iota(jnp.int32, wide.shape, 1)
    kept = jnp.where((col + WIN - HALF) % WIN == row % WIN, wide, 0.0).astype(jnp.bfloat16)
    place = (lax.broadcasted_iota(jnp.int32, (windows, cols), 1) + cols - HALF) % cols // WIN
    here = place == lax.broadcasted_iota(jnp.int32, (windows, cols), 0)
    here = jnp.where(here, 1.0, 0.0).astype(jnp.bfloat16)
    k_regions = lax.dot_general(kept, here, NT, preferred_element_type=jnp.float32)
    q_rows = jnp.concatenate([kept[:PER]] * GROUP, axis=0)
    q_regions = lax.dot_general(here, q_rows, NT, preferred_element_type=jnp.float32)
    return q_regions, k_regions


def finish_slot(embedded, mixed, w_out, gain):
    updated = embedded.astype(jnp.float32) + jnp.dot(
        mixed, w_out, preferred_element_type=jnp.float32
    )
    return from_windows(layer_norm(updated, gain)).astype(jnp.bfloat16)


def decode_slot(patches, final, w_dec_t):
    return (
        patches.astype(jnp.float32)
        + lax.dot_general(
            final, w_dec_t, (((1,), (1,)), ((), ())), preferred_element_type=jnp.float32
        )
    ).astype(jnp.bfloat16)


def fused_kernel(
    sample_ref,
    region_ref,
    a_gain_ref,
    o_gain_ref,
    store_ref,
    w_embed_ref,
    w_qkv_ref,
    w_out_ref,
    w_dec_ref,
    new_ref,
    patches,
    w_embed,
    w_qkv,
    w_out,
    w_dec,
    embedded,
    own,
    far,
    own_qkv,
    slot_sems,
    weight_sems,
    out_sems,
    send_sems,
    recv_sems,
):
    slots, rows_here, cols, patch_len = store_ref.shape
    lon_count = lax.axis_size("lon")
    strips = lax.axis_size("lat") * lon_count
    mine = lax.axis_index("lat") * lon_count + lax.axis_index("lon")
    other = lax.rem(mine + 2 * lax.rem(mine, 2) - 1 + strips, strips)
    partner = {"lat": lax.div(other, lon_count), "lon": lax.rem(other, lon_count)}

    def slot_in(s):
        return pltpu.make_async_copy(store_ref.at[s], patches.at[s], slot_sems.at[s])

    def slot_out(s):
        return pltpu.make_async_copy(patches.at[s], new_ref.at[s], out_sems.at[s])

    def send(s):
        return pltpu.make_async_remote_copy(
            src_ref=own.at[s],
            dst_ref=far.at[s],
            send_sem=send_sems.at[s],
            recv_sem=recv_sems.at[s],
            device_id=partner,
            device_id_type=pl.DeviceIdType.MESH,
        )

    weights = [
        pltpu.make_async_copy(src, dst, weight_sems.at[i])
        for i, (src, dst) in enumerate(
            ((w_embed_ref, w_embed), (w_qkv_ref, w_qkv), (w_out_ref, w_out), (w_dec_ref, w_dec))
        )
    ]
    slot_in(0).start()
    weights[0].start()
    for s in range(1, slots):
        slot_in(s).start()
    for copy in weights[1:]:
        copy.start()

    barrier = pltpu.get_barrier_semaphore()
    pl.semaphore_signal(
        barrier, inc=1, device_id=partner, device_id_type=pl.DeviceIdType.MESH
    )
    q_regions, k_regions = region_tables(
        region_ref[pl.ds(mine * HALF, HALF), :].astype(jnp.float32),
        region_ref[pl.ds(other * HALF, HALF), :].astype(jnp.float32),
    )
    pl.semaphore_wait(barrier, 1)
    weights[0].wait()

    @pl.loop(0, slots)
    def _(s):
        slot_in(s).wait()
        flat = patches[s].reshape(rows_here * cols, patch_len)
        embedded[s], own[s] = embed_slot(flat, w_embed[...], a_gain_ref[...])
        send(s).start()

    weights[1].wait()

    @pl.loop(0, slots)
    def _(s):
        query = jnp.dot(own[s], w_qkv[:, :D], preferred_element_type=jnp.float32)
        own_qkv[s, :, :D] = (query * (1.0 / math.sqrt(HDIM))).astype(jnp.bfloat16)
        own_qkv[s, :, D:] = jnp.dot(
            own[s], w_qkv[:, D:], preferred_element_type=jnp.float32
        ).astype(jnp.bfloat16)

    weights[2].wait()
    weights[3].wait()

    @pl.loop(0, slots)
    def _(s):
        send(s).wait()
        kv_other = jnp.dot(far[s], w_qkv[:, D:], preferred_element_type=jnp.float32)
        mixed = attend_slot(
            own_qkv[s, :, :D],
            own_qkv[s, :, D:],
            kv_other.astype(jnp.bfloat16),
            q_regions,
            k_regions,
        )
        final = finish_slot(embedded[s], mixed, w_out[...], o_gain_ref[...])
        slot = lax.axis_index("buf") * slots + s
        taken = sample_ref[0] == slot
        for b in range(1, sample_ref.shape[0]):
            taken = jnp.logical_or(taken, sample_ref[b] == slot)
        final = jnp.where(taken, final, jnp.zeros_like(final))
        flat = patches[s].reshape(rows_here * cols, patch_len)
        patches[s] = decode_slot(flat, final, w_dec[...]).reshape(rows_here, cols, patch_len)
        slot_out(s).start()

    @pl.loop(0, slots)
    def _(s):
        slot_out(s).wait()


def local_strips(store, sample_index, region_ids, w_embed, attn_gain, w_qkv, w_out, out_gain, w_dec):
    slots, rows_here, cols, patch_len = store.shape
    tokens = rows_here * cols
    held = lambda *shape: pltpu.VMEM(shape, jnp.bfloat16)
    vmem = pl.BlockSpec(memory_space=pltpu.VMEM)
    hbm = pl.BlockSpec(memory_space=pl.ANY)
    return pl.pallas_call(
        fused_kernel,
        in_specs=[pl.BlockSpec(memory_space=pltpu.SMEM), vmem, vmem, vmem] + [hbm] * 5,
        out_specs=hbm,
        out_shape=jax.ShapeDtypeStruct(store.shape, store.dtype),
        scratch_shapes=[
            held(*store.shape),
            held(*w_embed.shape),
            held(*w_qkv.shape),
            held(*w_out.shape),
            held(*w_dec.shape[::-1]),
            held(slots, tokens, D),
            held(slots, tokens, D),
            held(slots, tokens, D),
            held(slots, tokens, 3 * D),
            pltpu.SemaphoreType.DMA((slots,)),
            pltpu.SemaphoreType.DMA((4,)),
            pltpu.SemaphoreType.DMA((slots,)),
            pltpu.SemaphoreType.DMA((slots,)),
            pltpu.SemaphoreType.DMA((slots,)),
        ],
        compiler_params=pltpu.CompilerParams(
            vmem_limit_bytes=VMEM_LIMIT, collective_id=0, has_side_effects=True
        ),
    )(
        sample_index,
        region_ids,
        attn_gain[None],
        out_gain[None],
        store,
        w_embed,
        w_qkv,
        w_out,
        w_dec.T,
    )


def local(store, *rest):
    return (local_strips if store.shape[1] == HALF else local_tiles)(store, *rest)


def solution(mesh):
    return jax.shard_map(
        local,
        mesh=mesh,
        in_specs=(P("buf", ("lat", "lon"), None, None), P(), P(), P(), P(), P(), P(), P(), P()),
        out_specs=P("buf", ("lat", "lon"), None, None),
        check_vma=False,
    )
```

```python
import functools
import math

import jax
import jax.numpy as jnp
from jax import lax
from jax.experimental import pallas as pl
from jax.experimental.pallas import tpu as pltpu
from jax.sharding import PartitionSpec as P

D = 512
HEADS = 8
HDIM = 64
WIN = 8
HALF = WIN // 2
VMEM_LIMIT = 56 * 1024 * 1024
PICK_LIMIT = 4 * 1024 * 1024


def with_halo(array, sides, width):
    for axis, dim in sides:
        devices, length = (lax.axis_size(axis), array.shape[dim])
        up = [(i, (i + 1) % devices) for i in range(devices)]
        down = [(j, i) for i, j in up]
        last = lax.slice_in_dim(array, length - width, length, axis=dim)
        leading = lax.slice_in_dim(array, 0, width, axis=dim)
        before = lax.ppermute(last, axis, up)
        after = lax.ppermute(leading, axis, down)
        array = jnp.concatenate([before, array, after], axis=dim)
    return array


def layer_norm(values, gain_row):
    center = jnp.mean(values, axis=-1, keepdims=True)
    spread = jnp.mean(jnp.square(values - center), axis=-1, keepdims=True)
    return (values - center) * lax.rsqrt(spread + 1e-05) * gain_row


def window_mix(windows, regions):
    scores = jnp.einsum(
        "bwqhd,bwkhd->bwhqk",
        windows[:, :, :, 0],
        windows[:, :, :, 1],
        preferred_element_type=jnp.float32,
    ) / math.sqrt(HDIM)
    visible = (regions[:, :, None] == regions[:, None, :])[None, :, None]
    scores = jnp.where(visible, scores, -1e30)
    highest = jnp.max(scores, axis=-1, keepdims=True)
    expo_terms = jnp.where(visible, jnp.exp(scores - highest), 0.0)
    weights = (expo_terms / jnp.sum(expo_terms, axis=-1, keepdims=True)).astype(jnp.bfloat16)
    return jnp.einsum(
        "bwhqk,bwkhd->bwqhd", weights, windows[:, :, :, 2], preferred_element_type=jnp.float32
    ).astype(jnp.bfloat16)


def local_tiles(store, sample_index, region_ids, w_embed, attn_gain, w_qkv, w_out, out_gain, w_dec):
    lon_count = lax.axis_size("lon")
    slots_here, rows_here, width_all, patch_len = store.shape
    patch_cols = width_all // lon_count
    patch_rows = rows_here * lon_count
    half_win = WIN // 2
    ext_rows = patch_rows + WIN
    ext_cols = patch_cols + WIN
    own_slots = lax.axis_index("buf") * slots_here + jnp.arange(slots_here, dtype=jnp.int32)
    matches = own_slots[:, None] == sample_index[None, :]
    occupied = jnp.any(matches, axis=1)
    local_rows = store.reshape(slots_here, 1, rows_here, lon_count, patch_cols, patch_len)
    tile_data = lax.all_to_all(local_rows, "lon", split_axis=3, concat_axis=1, tiled=True)
    patches = tile_data.reshape(-1, patch_len)
    embedded = jnp.dot(patches, w_embed, preferred_element_type=jnp.float32).astype(jnp.bfloat16)
    normed = layer_norm(embedded.astype(jnp.float32), attn_gain).astype(jnp.bfloat16)
    normed = normed.reshape(slots_here, patch_rows, patch_cols, D)
    widened = with_halo(normed, (("lat", 1), ("lon", 2)), half_win)
    projected = jnp.dot(widened.reshape(-1, D), w_qkv, preferred_element_type=jnp.float32).astype(
        jnp.bfloat16
    )
    windows = projected.reshape(
        slots_here, ext_rows // WIN, WIN, ext_cols // WIN, WIN, 3, HEADS, HDIM
    )
    windows = windows.transpose(0, 1, 3, 2, 4, 5, 6, 7).reshape(
        slots_here, -1, WIN * WIN, 3, HEADS, HDIM
    )
    total_rows, total_cols = region_ids.shape
    row_pick = (
        lax.axis_index("lat") * patch_rows - half_win + jnp.arange(ext_rows, dtype=jnp.int32)
    ) % total_rows
    col_pick = (
        lax.axis_index("lon") * patch_cols - half_win + jnp.arange(ext_cols, dtype=jnp.int32)
    ) % total_cols
    local_regions = jnp.take(jnp.take(region_ids, row_pick, axis=0), col_pick, axis=1)
    region_windows = (
        local_regions.reshape(ext_rows // WIN, WIN, ext_cols // WIN, WIN)
        .transpose(0, 2, 1, 3)
        .reshape(-1, WIN * WIN)
    )
    mixed_heads = window_mix(windows, region_windows)
    placed = mixed_heads.reshape(slots_here, ext_rows // WIN, ext_cols // WIN, WIN, WIN, D)
    placed = placed.transpose(0, 1, 3, 2, 4, 5).reshape(slots_here, ext_rows, ext_cols, D)
    placed = placed[:, half_win : half_win + patch_rows, half_win : half_win + patch_cols].reshape(
        -1, D
    )
    updated = embedded.astype(jnp.float32) + jnp.dot(
        placed, w_out, preferred_element_type=jnp.float32
    )
    final_norm = layer_norm(updated, out_gain).astype(jnp.bfloat16)
    predicted = (
        patches.astype(jnp.float32) + jnp.dot(final_norm, w_dec, preferred_element_type=jnp.float32)
    ).astype(jnp.bfloat16)
    outgoing = predicted.reshape(slots_here, lon_count, rows_here, 1, patch_cols, patch_len)
    returned = lax.all_to_all(outgoing, "lon", split_axis=1, concat_axis=3, tiled=True)
    strip_data = returned.reshape(slots_here, rows_here, width_all, patch_len)
    return jnp.where(occupied[:, None, None, None], strip_data, store)


def to_windows(values):
    rows, cols = HALF, values.shape[0] // HALF
    parts = [pltpu.roll(values[cols * i : cols * (i + 1)], cols - HALF, 0) for i in range(rows)]
    return jnp.concatenate(
        [parts[i][WIN * c : WIN * (c + 1)] for c in range(cols // WIN) for i in range(rows)], axis=0
    )


def from_windows(values):
    rows, cols = HALF, values.shape[0] // HALF
    parts = []
    for i in range(rows):
        line = jnp.concatenate(
            [
                values[WIN * (rows * c + i) : WIN * (rows * c + i + 1)]
                for c in range(cols // WIN)
            ],
            axis=0,
        )
        parts.append(pltpu.roll(line, HALF, 0))
    return jnp.concatenate(parts, axis=0)


def embed_slot(patches, w_embed, gain):
    embedded = jnp.dot(patches, w_embed, preferred_element_type=jnp.float32).astype(jnp.bfloat16)
    embedded = to_windows(embedded.astype(jnp.float32))
    normed = layer_norm(embedded, gain).astype(jnp.bfloat16)
    return embedded.astype(jnp.bfloat16), normed


NT = (((1,), (1,)), ((), ()))
TN = (((0,), (0,)), ((), ()))
GROUP = 4
WIDE = GROUP * HDIM
PER = WIN * HALF


def attend_slot(query, kv_own, kv_other, q_regions, k_regions):
    shape = (GROUP * PER, WIDE)
    pick = (
        lax.broadcasted_iota(jnp.int32, shape, 0) // PER
        == lax.broadcasted_iota(jnp.int32, shape, 1) // HDIM
    )
    head_mask = jnp.where(pick, 1.0, 0.0).astype(jnp.bfloat16)
    windows = query.shape[0] // PER
    kvs, scores, weights, mixed = [], [], [], []
    for c in range(windows):
        at = slice(PER * c, PER * (c + 1))
        kvs.append(jnp.concatenate([kv_own[at], kv_other[at]], axis=0))
        for g in range(HEADS // GROUP):
            cols = slice(WIDE * g, WIDE * (g + 1))
            queries = jnp.concatenate([query[at, cols]] * GROUP, axis=0) * head_mask
            scores.append(
                lax.dot_general(kvs[c][:, cols], queries, NT, preferred_element_type=jnp.float32)
            )
    for c in range(windows):
        seen = k_regions[:, c : c + 1] == q_regions[c : c + 1, :]
        for g in range(HEADS // GROUP):
            part = jnp.where(seen, scores[2 * c + g], -1e30)
            expo = jnp.exp(part - jnp.max(part, axis=0, keepdims=True))
            total = jnp.sum(expo, axis=0, keepdims=True)
            weights.append((expo * (1.0 / total)).astype(jnp.bfloat16))
    for c in range(windows):
        groups = []
        for g in range(HEADS // GROUP):
            heads = lax.dot_general(
                weights[2 * c + g],
                kvs[c][:, D + WIDE * g : D + WIDE * (g + 1)],
                TN,
                preferred_element_type=jnp.float32,
            )
            heads = jnp.where(pick, heads, 0.0)
            total = heads[:PER]
            for h in range(1, GROUP):
                total = total + heads[PER * h : PER * (h + 1)]
            groups.append(total)
        mixed.append(jnp.concatenate(groups, axis=1).astype(jnp.bfloat16))
    return jnp.concatenate(mixed, axis=0)


def region_tables(own, far):
    rows, cols = own.shape
    windows = cols // WIN
    lines = [own[i : i + 1] for i in range(rows)] + [far[i : i + 1] for i in range(rows)]
    wide = jnp.concatenate([jnp.broadcast_to(line, (WIN, cols)) for line in lines], axis=0)
    row = lax.broadcasted_iota(jnp.int32, wide.shape, 0)
    col = lax.broadcasted_iota(jnp.int32, wide.shape, 1)
    kept = jnp.where((col + WIN - HALF) % WIN == row % WIN, wide, 0.0).astype(jnp.bfloat16)
    place = (lax.broadcasted_iota(jnp.int32, (windows, cols), 1) + cols - HALF) % cols // WIN
    here = place == lax.broadcasted_iota(jnp.int32, (windows, cols), 0)
    here = jnp.where(here, 1.0, 0.0).astype(jnp.bfloat16)
    k_regions = lax.dot_general(kept, here, NT, preferred_element_type=jnp.float32)
    q_rows = jnp.concatenate([kept[:PER]] * GROUP, axis=0)
    q_regions = lax.dot_general(here, q_rows, NT, preferred_element_type=jnp.float32)
    return q_regions, k_regions


def finish_part(embedded, mixed, w_out, gain):
    updated = embedded.astype(jnp.float32) + jnp.dot(
        mixed, w_out, preferred_element_type=jnp.float32
    )
    return layer_norm(updated, gain)


def decode_slot(patches, final, w_dec_t):
    return (
        patches.astype(jnp.float32)
        + lax.dot_general(
            final, w_dec_t, (((1,), (1,)), ((), ())), preferred_element_type=jnp.float32
        )
    ).astype(jnp.bfloat16)


def taken_slots(sample_ref, slots):
    first = lax.axis_index("buf") * slots
    taken = []
    for s in range(slots):
        found = sample_ref[0] == first + s
        for b in range(1, sample_ref.shape[0]):
            found = jnp.logical_or(found, sample_ref[b] == first + s)
        taken.append(jnp.where(found, 1, 0))
    ranks = [sum(taken[:s], jnp.int32(0)) for s in range(slots)]
    return taken, ranks


def fused_kernel(
    count,
    sample_ref,
    region_ref,
    a_gain_ref,
    o_gain_ref,
    store_ref,
    w_embed_ref,
    w_qkv_ref,
    w_out_ref,
    w_dec_ref,
    new_ref,
    patches,
    w_embed,
    w_qkv,
    w_out,
    w_dec,
    embedded,
    own,
    far,
    own_qkv,
    finals,
    result,
    slot_sems,
    weight_sems,
    out_sems,
    send_sems,
    recv_sems,
):
    slots, rows_here, cols, patch_len = store_ref.shape
    lon_count = lax.axis_size("lon")
    strips = lax.axis_size("lat") * lon_count
    mine = lax.axis_index("lat") * lon_count + lax.axis_index("lon")
    other = lax.rem(mine + 2 * lax.rem(mine, 2) - 1 + strips, strips)
    partner = {"lat": lax.div(other, lon_count), "lon": lax.rem(other, lon_count)}

    def slot_in(s):
        return pltpu.make_async_copy(store_ref.at[s], patches.at[s], slot_sems.at[s])

    def slot_out(s):
        return pltpu.make_async_copy(result.at[s], new_ref.at[s], out_sems.at[s])

    tokens = rows_here * cols
    half = tokens // 2
    halves = [pl.ds(half * h, half) for h in range(2)]

    def send(k, h):
        return pltpu.make_async_remote_copy(
            src_ref=own.at[k, halves[h]],
            dst_ref=far.at[k, halves[h]],
            send_sem=send_sems.at[k, h],
            recv_sem=recv_sems.at[k, h],
            device_id=partner,
            device_id_type=pl.DeviceIdType.MESH,
        )

    weights = [
        pltpu.make_async_copy(src, dst, weight_sems.at[i])
        for i, (src, dst) in enumerate(
            ((w_embed_ref, w_embed), (w_qkv_ref, w_qkv), (w_out_ref, w_out), (w_dec_ref, w_dec))
        )
    ]
    slot_in(0).start()
    weights[0].start()
    for s in range(1, slots):
        slot_in(s).start()
    for copy in weights[1:]:
        copy.start()

    barrier = pltpu.get_barrier_semaphore()
    pl.semaphore_signal(
        barrier, inc=1, device_id=partner, device_id_type=pl.DeviceIdType.MESH
    )
    q_regions, k_regions = region_tables(
        region_ref[pl.ds(mine * HALF, HALF), :].astype(jnp.float32),
        region_ref[pl.ds(other * HALF, HALF), :].astype(jnp.float32),
    )
    pl.semaphore_wait(barrier, 1)
    compact = count < slots
    taken, ranks = taken_slots(sample_ref, slots)

    def slot_of(k):
        if not compact:
            return k
        slot = jnp.int32(0)
        for s in range(slots):
            slot += jnp.where(jnp.logical_and(taken[s] == 1, ranks[s] == k), s, 0)
        return slot

    weights[0].wait()
    if compact:
        for s in range(slots):
            slot_in(s).wait()

    @pl.loop(0, count)
    def _(k):
        if not compact:
            slot_in(k).wait()
        flat = patches[slot_of(k)].reshape(tokens, patch_len)
        embedded[k], own[k] = embed_slot(flat, w_embed[...], a_gain_ref[...])
        for h in range(2):
            send(k, h).start()

    weights[1].wait()

    @pl.loop(0, count)
    def _(k):
        query = jnp.dot(own[k], w_qkv[:, :D], preferred_element_type=jnp.float32)
        own_qkv[k, :, :D] = (query * (1.0 / math.sqrt(HDIM))).astype(jnp.bfloat16)
        own_qkv[k, :, D:] = jnp.dot(
            own[k], w_qkv[:, D:], preferred_element_type=jnp.float32
        ).astype(jnp.bfloat16)

    weights[2].wait()
    weights[3].wait()
    windows = tokens // PER

    @pl.loop(0, count)
    def _(k):
        for h in range(2):
            send(k, h).wait()
            at = slice(half * h, half * (h + 1))
            here = slice(windows // 2 * h, windows // 2 * (h + 1))
            kv_other = jnp.dot(far[k, at], w_qkv[:, D:], preferred_element_type=jnp.float32)
            mixed = attend_slot(
                own_qkv[k, at, :D],
                own_qkv[k, at, D:],
                kv_other.astype(jnp.bfloat16),
                q_regions[here],
                k_regions[:, here],
            )
            finals[at] = finish_part(embedded[k, at], mixed, w_out[...], o_gain_ref[...])
        final = from_windows(finals[...]).astype(jnp.bfloat16)
        flat = patches[slot_of(k)].reshape(tokens, patch_len)
        result[k] = decode_slot(flat, final, w_dec[...]).reshape(rows_here, cols, patch_len)
        slot_out(k).start()

    @pl.loop(0, count)
    def _(k):
        slot_out(k).wait()


def pick_kernel(sample_ref, result_ref, store_ref, new_ref, sems):
    slots = store_ref.shape[0]
    compact = result_ref.shape[0] < slots
    taken, ranks = taken_slots(sample_ref, slots)
    for s in range(slots):

        @pl.when(taken[s] == 1)
        def _():
            source = result_ref.at[ranks[s] if compact else s]
            pltpu.make_async_copy(source, new_ref.at[s], sems.at[s]).start()

        @pl.when(taken[s] == 0)
        def _():
            pltpu.make_async_copy(store_ref.at[s], new_ref.at[s], sems.at[s]).start()

    for s in range(slots):
        pltpu.make_async_copy(store_ref.at[s], new_ref.at[s], sems.at[s]).wait()


def strips_step(
    count, store, sample_index, region_ids, w_embed, attn_gain, w_qkv, w_out, out_gain, w_dec
):
    slots, rows_here, cols, patch_len = store.shape
    tokens = rows_here * cols
    held = lambda *shape: pltpu.VMEM(shape, jnp.bfloat16)
    vmem = pl.BlockSpec(memory_space=pltpu.VMEM)
    hbm = pl.BlockSpec(memory_space=pl.ANY)
    smem = pl.BlockSpec(memory_space=pltpu.SMEM)
    result = pl.pallas_call(
        functools.partial(fused_kernel, count),
        in_specs=[smem, vmem, vmem, vmem] + [hbm] * 5,
        out_specs=hbm,
        out_shape=pltpu.VMEM((count, *store.shape[1:]), store.dtype),
        scratch_shapes=[
            held(*store.shape),
            held(*w_embed.shape),
            held(*w_qkv.shape),
            held(*w_out.shape),
            held(*w_dec.shape[::-1]),
            held(count, tokens, D),
            held(count, tokens, D),
            held(count, tokens, D),
            held(count, tokens, 3 * D),
            pltpu.VMEM((tokens, D), jnp.float32),
            held(count, *store.shape[1:]),
            pltpu.SemaphoreType.DMA((slots,)),
            pltpu.SemaphoreType.DMA((4,)),
            pltpu.SemaphoreType.DMA((count,)),
            pltpu.SemaphoreType.DMA((count, 2)),
            pltpu.SemaphoreType.DMA((count, 2)),
        ],
        compiler_params=pltpu.CompilerParams(
            vmem_limit_bytes=VMEM_LIMIT, collective_id=slots - count, has_side_effects=True
        ),
    )(
        sample_index,
        region_ids,
        attn_gain[None],
        out_gain[None],
        store,
        w_embed,
        w_qkv,
        w_out,
        w_dec.T,
    )
    return pl.pallas_call(
        pick_kernel,
        in_specs=[smem, hbm, hbm],
        out_specs=hbm,
        out_shape=jax.ShapeDtypeStruct(store.shape, store.dtype),
        scratch_shapes=[pltpu.SemaphoreType.DMA((slots,))],
        compiler_params=pltpu.CompilerParams(vmem_limit_bytes=PICK_LIMIT),
    )(sample_index, result, store)


def local_strips(store, *rest):
    return strips_step(store.shape[0], store, *rest)


def local(store, *rest):
    return (local_strips if store.shape[1] == HALF else local_tiles)(store, *rest)


def solution(mesh):
    return jax.shard_map(
        local,
        mesh=mesh,
        in_specs=(P("buf", ("lat", "lon"), None, None), P(), P(), P(), P(), P(), P(), P(), P()),
        out_specs=P("buf", ("lat", "lon"), None, None),
        check_vma=False,
    )
```

```python
import functools
import math

import jax
import jax.numpy as jnp
from jax import lax
from jax.experimental import pallas as pl
from jax.experimental.pallas import tpu as pltpu
from jax.sharding import PartitionSpec as P

D = 512
HEADS = 8
HDIM = 64
WIN = 8
HALF = WIN // 2
VMEM_LIMIT = 56 * 1024 * 1024
PICK_LIMIT = 4 * 1024 * 1024


def with_halo(array, sides, width):
    for axis, dim in sides:
        devices, length = (lax.axis_size(axis), array.shape[dim])
        up = [(i, (i + 1) % devices) for i in range(devices)]
        down = [(j, i) for i, j in up]
        last = lax.slice_in_dim(array, length - width, length, axis=dim)
        leading = lax.slice_in_dim(array, 0, width, axis=dim)
        before = lax.ppermute(last, axis, up)
        after = lax.ppermute(leading, axis, down)
        array = jnp.concatenate([before, array, after], axis=dim)
    return array


def layer_norm(values, gain_row):
    center = jnp.mean(values, axis=-1, keepdims=True)
    spread = jnp.mean(jnp.square(values - center), axis=-1, keepdims=True)
    return (values - center) * lax.rsqrt(spread + 1e-05) * gain_row


def window_mix(windows, regions):
    scores = jnp.einsum(
        "bwqhd,bwkhd->bwhqk",
        windows[:, :, :, 0],
        windows[:, :, :, 1],
        preferred_element_type=jnp.float32,
    ) / math.sqrt(HDIM)
    visible = (regions[:, :, None] == regions[:, None, :])[None, :, None]
    scores = jnp.where(visible, scores, -1e30)
    highest = jnp.max(scores, axis=-1, keepdims=True)
    expo_terms = jnp.where(visible, jnp.exp(scores - highest), 0.0)
    weights = (expo_terms / jnp.sum(expo_terms, axis=-1, keepdims=True)).astype(jnp.bfloat16)
    return jnp.einsum(
        "bwhqk,bwkhd->bwqhd", weights, windows[:, :, :, 2], preferred_element_type=jnp.float32
    ).astype(jnp.bfloat16)


def local_tiles(store, sample_index, region_ids, w_embed, attn_gain, w_qkv, w_out, out_gain, w_dec):
    lon_count = lax.axis_size("lon")
    slots_here, rows_here, width_all, patch_len = store.shape
    patch_cols = width_all // lon_count
    patch_rows = rows_here * lon_count
    half_win = WIN // 2
    ext_rows = patch_rows + WIN
    ext_cols = patch_cols + WIN
    own_slots = lax.axis_index("buf") * slots_here + jnp.arange(slots_here, dtype=jnp.int32)
    matches = own_slots[:, None] == sample_index[None, :]
    occupied = jnp.any(matches, axis=1)
    local_rows = store.reshape(slots_here, 1, rows_here, lon_count, patch_cols, patch_len)
    tile_data = lax.all_to_all(local_rows, "lon", split_axis=3, concat_axis=1, tiled=True)
    patches = tile_data.reshape(-1, patch_len)
    embedded = jnp.dot(patches, w_embed, preferred_element_type=jnp.float32).astype(jnp.bfloat16)
    normed = layer_norm(embedded.astype(jnp.float32), attn_gain).astype(jnp.bfloat16)
    normed = normed.reshape(slots_here, patch_rows, patch_cols, D)
    widened = with_halo(normed, (("lat", 1), ("lon", 2)), half_win)
    projected = jnp.dot(widened.reshape(-1, D), w_qkv, preferred_element_type=jnp.float32).astype(
        jnp.bfloat16
    )
    windows = projected.reshape(
        slots_here, ext_rows // WIN, WIN, ext_cols // WIN, WIN, 3, HEADS, HDIM
    )
    windows = windows.transpose(0, 1, 3, 2, 4, 5, 6, 7).reshape(
        slots_here, -1, WIN * WIN, 3, HEADS, HDIM
    )
    total_rows, total_cols = region_ids.shape
    row_pick = (
        lax.axis_index("lat") * patch_rows - half_win + jnp.arange(ext_rows, dtype=jnp.int32)
    ) % total_rows
    col_pick = (
        lax.axis_index("lon") * patch_cols - half_win + jnp.arange(ext_cols, dtype=jnp.int32)
    ) % total_cols
    local_regions = jnp.take(jnp.take(region_ids, row_pick, axis=0), col_pick, axis=1)
    region_windows = (
        local_regions.reshape(ext_rows // WIN, WIN, ext_cols // WIN, WIN)
        .transpose(0, 2, 1, 3)
        .reshape(-1, WIN * WIN)
    )
    mixed_heads = window_mix(windows, region_windows)
    placed = mixed_heads.reshape(slots_here, ext_rows // WIN, ext_cols // WIN, WIN, WIN, D)
    placed = placed.transpose(0, 1, 3, 2, 4, 5).reshape(slots_here, ext_rows, ext_cols, D)
    placed = placed[:, half_win : half_win + patch_rows, half_win : half_win + patch_cols].reshape(
        -1, D
    )
    updated = embedded.astype(jnp.float32) + jnp.dot(
        placed, w_out, preferred_element_type=jnp.float32
    )
    final_norm = layer_norm(updated, out_gain).astype(jnp.bfloat16)
    predicted = (
        patches.astype(jnp.float32) + jnp.dot(final_norm, w_dec, preferred_element_type=jnp.float32)
    ).astype(jnp.bfloat16)
    outgoing = predicted.reshape(slots_here, lon_count, rows_here, 1, patch_cols, patch_len)
    returned = lax.all_to_all(outgoing, "lon", split_axis=1, concat_axis=3, tiled=True)
    strip_data = returned.reshape(slots_here, rows_here, width_all, patch_len)
    return jnp.where(occupied[:, None, None, None], strip_data, store)


def to_windows(values):
    rows, cols = HALF, values.shape[0] // HALF
    parts = [pltpu.roll(values[cols * i : cols * (i + 1)], cols - HALF, 0) for i in range(rows)]
    return jnp.concatenate(
        [parts[i][WIN * c : WIN * (c + 1)] for c in range(cols // WIN) for i in range(rows)], axis=0
    )


def from_windows(values):
    rows, cols = HALF, values.shape[0] // HALF
    parts = []
    for i in range(rows):
        line = jnp.concatenate(
            [
                values[WIN * (rows * c + i) : WIN * (rows * c + i + 1)]
                for c in range(cols // WIN)
            ],
            axis=0,
        )
        parts.append(pltpu.roll(line, HALF, 0))
    return jnp.concatenate(parts, axis=0)


def embed_slot(patches, w_embed, gain):
    embedded = jnp.dot(patches, w_embed, preferred_element_type=jnp.float32).astype(jnp.bfloat16)
    embedded = to_windows(embedded.astype(jnp.float32))
    normed = layer_norm(embedded, gain).astype(jnp.bfloat16)
    return embedded.astype(jnp.bfloat16), normed


NT = (((1,), (1,)), ((), ()))
TN = (((0,), (0,)), ((), ()))
GROUP = 4
WIDE = GROUP * HDIM
PER = WIN * HALF


def attend_slot(query, kv_own, kv_other, q_regions, k_regions):
    shape = (GROUP * PER, WIDE)
    pick = (
        lax.broadcasted_iota(jnp.int32, shape, 0) // PER
        == lax.broadcasted_iota(jnp.int32, shape, 1) // HDIM
    )
    head_mask = jnp.where(pick, 1.0, 0.0).astype(jnp.bfloat16)
    windows = query.shape[0] // PER
    kvs, scores, weights, mixed = [], [], [], []
    for c in range(windows):
        at = slice(PER * c, PER * (c + 1))
        kvs.append(jnp.concatenate([kv_own[at], kv_other[at]], axis=0))
        for g in range(HEADS // GROUP):
            cols = slice(WIDE * g, WIDE * (g + 1))
            queries = jnp.concatenate([query[at, cols]] * GROUP, axis=0) * head_mask
            scores.append(
                lax.dot_general(kvs[c][:, cols], queries, NT, preferred_element_type=jnp.float32)
            )
    for c in range(windows):
        seen = k_regions[:, c : c + 1] == q_regions[c : c + 1, :]
        for g in range(HEADS // GROUP):
            part = jnp.where(seen, scores[2 * c + g], -1e30)
            expo = jnp.exp(part - jnp.max(part, axis=0, keepdims=True))
            total = jnp.sum(expo, axis=0, keepdims=True)
            weights.append((expo * (1.0 / total)).astype(jnp.bfloat16))
    for c in range(windows):
        groups = []
        for g in range(HEADS // GROUP):
            heads = lax.dot_general(
                weights[2 * c + g],
                kvs[c][:, D + WIDE * g : D + WIDE * (g + 1)],
                TN,
                preferred_element_type=jnp.float32,
            )
            heads = jnp.where(pick, heads, 0.0)
            total = heads[:PER]
            for h in range(1, GROUP):
                total = total + heads[PER * h : PER * (h + 1)]
            groups.append(total)
        mixed.append(jnp.concatenate(groups, axis=1).astype(jnp.bfloat16))
    return jnp.concatenate(mixed, axis=0)


def region_tables(own, far):
    rows, cols = own.shape
    windows = cols // WIN
    lines = [own[i : i + 1] for i in range(rows)] + [far[i : i + 1] for i in range(rows)]
    wide = jnp.concatenate([jnp.broadcast_to(line, (WIN, cols)) for line in lines], axis=0)
    row = lax.broadcasted_iota(jnp.int32, wide.shape, 0)
    col = lax.broadcasted_iota(jnp.int32, wide.shape, 1)
    kept = jnp.where((col + WIN - HALF) % WIN == row % WIN, wide, 0.0).astype(jnp.bfloat16)
    place = (lax.broadcasted_iota(jnp.int32, (windows, cols), 1) + cols - HALF) % cols // WIN
    here = place == lax.broadcasted_iota(jnp.int32, (windows, cols), 0)
    here = jnp.where(here, 1.0, 0.0).astype(jnp.bfloat16)
    k_regions = lax.dot_general(kept, here, NT, preferred_element_type=jnp.float32)
    q_rows = jnp.concatenate([kept[:PER]] * GROUP, axis=0)
    q_regions = lax.dot_general(here, q_rows, NT, preferred_element_type=jnp.float32)
    return q_regions, k_regions


def finish_part(embedded, mixed, w_out, gain):
    updated = embedded.astype(jnp.float32) + jnp.dot(
        mixed, w_out, preferred_element_type=jnp.float32
    )
    return layer_norm(updated, gain)


def decode_slot(patches, final, w_dec_t):
    return (
        patches.astype(jnp.float32)
        + lax.dot_general(
            final, w_dec_t, (((1,), (1,)), ((), ())), preferred_element_type=jnp.float32
        )
    ).astype(jnp.bfloat16)


def taken_slots(sample_ref, slots):
    first = lax.axis_index("buf") * slots
    taken = []
    for s in range(slots):
        found = sample_ref[0] == first + s
        for b in range(1, sample_ref.shape[0]):
            found = jnp.logical_or(found, sample_ref[b] == first + s)
        taken.append(jnp.where(found, 1, 0))
    ranks = [sum(taken[:s], jnp.int32(0)) for s in range(slots)]
    return taken, ranks


def fused_kernel(
    count,
    sample_ref,
    region_ref,
    a_gain_ref,
    o_gain_ref,
    store_ref,
    w_embed_ref,
    w_qkv_ref,
    w_out_ref,
    w_dec_ref,
    new_ref,
    patches,
    w_embed,
    w_qkv,
    w_out,
    w_dec,
    embedded,
    own,
    far,
    own_qkv,
    finals,
    result,
    slot_sems,
    weight_sems,
    out_sems,
    send_sems,
    recv_sems,
):
    slots, rows_here, cols, patch_len = store_ref.shape
    lon_count = lax.axis_size("lon")
    strips = lax.axis_size("lat") * lon_count
    mine = lax.axis_index("lat") * lon_count + lax.axis_index("lon")
    other = lax.rem(mine + 2 * lax.rem(mine, 2) - 1 + strips, strips)
    partner = {"lat": lax.div(other, lon_count), "lon": lax.rem(other, lon_count)}

    def slot_in(s):
        return pltpu.make_async_copy(store_ref.at[s], patches.at[s], slot_sems.at[s])

    def slot_out(s):
        return pltpu.make_async_copy(result.at[s], new_ref.at[s], out_sems.at[s])

    tokens = rows_here * cols
    half = tokens // 2
    halves = [pl.ds(half * h, half) for h in range(2)]

    def send(k, h):
        return pltpu.make_async_remote_copy(
            src_ref=own.at[k, halves[h]],
            dst_ref=far.at[k, halves[h]],
            send_sem=send_sems.at[k, h],
            recv_sem=recv_sems.at[k, h],
            device_id=partner,
            device_id_type=pl.DeviceIdType.MESH,
        )

    weights = [
        pltpu.make_async_copy(src, dst, weight_sems.at[i])
        for i, (src, dst) in enumerate(
            ((w_embed_ref, w_embed), (w_qkv_ref, w_qkv), (w_out_ref, w_out), (w_dec_ref, w_dec))
        )
    ]
    slot_in(0).start()
    weights[0].start()
    for s in range(1, slots):
        slot_in(s).start()
    for copy in weights[1:]:
        copy.start()

    barrier = pltpu.get_barrier_semaphore()
    pl.semaphore_signal(
        barrier, inc=1, device_id=partner, device_id_type=pl.DeviceIdType.MESH
    )
    q_regions, k_regions = region_tables(
        region_ref[pl.ds(mine * HALF, HALF), :].astype(jnp.float32),
        region_ref[pl.ds(other * HALF, HALF), :].astype(jnp.float32),
    )
    pl.semaphore_wait(barrier, 1)
    compact = count < slots
    taken, ranks = taken_slots(sample_ref, slots)

    def slot_of(k):
        if not compact:
            return k
        slot = jnp.int32(0)
        for s in range(slots):
            slot += jnp.where(jnp.logical_and(taken[s] == 1, ranks[s] == k), s, 0)
        return slot

    weights[0].wait()
    if compact:
        for s in range(slots):
            slot_in(s).wait()

    @pl.loop(0, count)
    def _(k):
        if not compact:
            slot_in(k).wait()
        flat = patches[slot_of(k)].reshape(tokens, patch_len)
        embedded[k], own[k] = embed_slot(flat, w_embed[...], a_gain_ref[...])
        for h in range(2):
            send(k, h).start()

    weights[1].wait()

    @pl.loop(0, count)
    def _(k):
        query = jnp.dot(own[k], w_qkv[:, :D], preferred_element_type=jnp.float32)
        own_qkv[k, :, :D] = (query * (1.0 / math.sqrt(HDIM))).astype(jnp.bfloat16)
        own_qkv[k, :, D:] = jnp.dot(
            own[k], w_qkv[:, D:], preferred_element_type=jnp.float32
        ).astype(jnp.bfloat16)

    weights[2].wait()
    weights[3].wait()
    windows = tokens // PER

    @pl.loop(0, count)
    def _(k):
        for h in range(2):
            send(k, h).wait()
            at = slice(half * h, half * (h + 1))
            here = slice(windows // 2 * h, windows // 2 * (h + 1))
            kv_other = jnp.dot(far[k, at], w_qkv[:, D:], preferred_element_type=jnp.float32)
            mixed = attend_slot(
                own_qkv[k, at, :D],
                own_qkv[k, at, D:],
                kv_other.astype(jnp.bfloat16),
                q_regions[here],
                k_regions[:, here],
            )
            finals[at] = finish_part(embedded[k, at], mixed, w_out[...], o_gain_ref[...])
        final = from_windows(finals[...]).astype(jnp.bfloat16)
        flat = patches[slot_of(k)].reshape(tokens, patch_len)
        result[k] = decode_slot(flat, final, w_dec[...]).reshape(rows_here, cols, patch_len)
        slot_out(k).start()

    @pl.loop(0, count)
    def _(k):
        slot_out(k).wait()


def is_even(samples, slots, fair, owners):
    even = True
    for owner in range(owners):
        held = jnp.int32(0)
        for b in range(samples.shape[0]):
            held += jnp.where(lax.div(samples[b], slots) == owner, 1, 0)
        even = jnp.logical_and(even, held <= fair)
    return even


def pick_kernel(sample_ref, result_ref, store_ref, new_ref, sems):
    slots = store_ref.shape[0]
    compact = result_ref.shape[0] < slots
    taken, ranks = taken_slots(sample_ref, slots)
    for s in range(slots):

        @pl.when(taken[s] == 1)
        def _():
            source = result_ref.at[ranks[s] if compact else s]
            pltpu.make_async_copy(source, new_ref.at[s], sems.at[s]).start()

        @pl.when(taken[s] == 0)
        def _():
            pltpu.make_async_copy(store_ref.at[s], new_ref.at[s], sems.at[s]).start()

    for s in range(slots):
        pltpu.make_async_copy(store_ref.at[s], new_ref.at[s], sems.at[s]).wait()


def strips_step(
    count, store, sample_index, region_ids, w_embed, attn_gain, w_qkv, w_out, out_gain, w_dec
):
    slots, rows_here, cols, patch_len = store.shape
    tokens = rows_here * cols
    held = lambda *shape: pltpu.VMEM(shape, jnp.bfloat16)
    vmem = pl.BlockSpec(memory_space=pltpu.VMEM)
    hbm = pl.BlockSpec(memory_space=pl.ANY)
    smem = pl.BlockSpec(memory_space=pltpu.SMEM)
    result = pl.pallas_call(
        functools.partial(fused_kernel, count),
        in_specs=[smem, vmem, vmem, vmem] + [hbm] * 5,
        out_specs=hbm,
        out_shape=pltpu.VMEM((count, *store.shape[1:]), store.dtype),
        scratch_shapes=[
            held(*store.shape),
            held(*w_embed.shape),
            held(*w_qkv.shape),
            held(*w_out.shape),
            held(*w_dec.shape[::-1]),
            held(count, tokens, D),
            held(count, tokens, D),
            held(count, tokens, D),
            held(count, tokens, 3 * D),
            pltpu.VMEM((tokens, D), jnp.float32),
            held(count, *store.shape[1:]),
            pltpu.SemaphoreType.DMA((slots,)),
            pltpu.SemaphoreType.DMA((4,)),
            pltpu.SemaphoreType.DMA((count,)),
            pltpu.SemaphoreType.DMA((count, 2)),
            pltpu.SemaphoreType.DMA((count, 2)),
        ],
        compiler_params=pltpu.CompilerParams(
            vmem_limit_bytes=VMEM_LIMIT, collective_id=slots - count, has_side_effects=True
        ),
    )(
        sample_index,
        region_ids,
        attn_gain[None],
        out_gain[None],
        store,
        w_embed,
        w_qkv,
        w_out,
        w_dec.T,
    )
    return pl.pallas_call(
        pick_kernel,
        in_specs=[smem, hbm, hbm],
        out_specs=hbm,
        out_shape=pltpu.HBM(store.shape, store.dtype),
        scratch_shapes=[pltpu.SemaphoreType.DMA((slots,))],
        compiler_params=pltpu.CompilerParams(vmem_limit_bytes=PICK_LIMIT),
    )(sample_index, result, store)


def local_strips(store, sample_index, *rest):
    slots = store.shape[0]
    owners = lax.axis_size("buf")
    fair = -(-sample_index.shape[0] // owners)
    if fair >= slots:
        return strips_step(slots, store, sample_index, *rest)
    return lax.cond(
        is_even(sample_index, slots, fair, owners),
        functools.partial(strips_step, fair),
        functools.partial(strips_step, slots),
        store,
        sample_index,
        *rest,
    )


def local(store, *rest):
    return (local_strips if store.shape[1] == HALF else local_tiles)(store, *rest)


def solution(mesh):
    return jax.shard_map(
        local,
        mesh=mesh,
        in_specs=(P("buf", ("lat", "lon"), None, None), P(), P(), P(), P(), P(), P(), P(), P()),
        out_specs=P("buf", ("lat", "lon"), None, None),
        check_vma=False,
    )
```

```python
import math

import jax
import jax.numpy as jnp
from jax import lax
from jax.experimental import pallas as pl
from jax.experimental.pallas import tpu as pltpu
from jax.sharding import PartitionSpec as P

D = 512
HEADS = 8
HDIM = 64
WIN = 8
HALF = WIN // 2
VMEM_LIMIT = 56 * 1024 * 1024
PICK_LIMIT = 4 * 1024 * 1024


def with_halo(array, sides, width):
    for axis, dim in sides:
        devices, length = (lax.axis_size(axis), array.shape[dim])
        up = [(i, (i + 1) % devices) for i in range(devices)]
        down = [(j, i) for i, j in up]
        last = lax.slice_in_dim(array, length - width, length, axis=dim)
        leading = lax.slice_in_dim(array, 0, width, axis=dim)
        before = lax.ppermute(last, axis, up)
        after = lax.ppermute(leading, axis, down)
        array = jnp.concatenate([before, array, after], axis=dim)
    return array


def layer_norm(values, gain_row):
    center = jnp.mean(values, axis=-1, keepdims=True)
    spread = jnp.mean(jnp.square(values - center), axis=-1, keepdims=True)
    return (values - center) * lax.rsqrt(spread + 1e-05) * gain_row


def window_mix(windows, regions):
    scores = jnp.einsum(
        "bwqhd,bwkhd->bwhqk",
        windows[:, :, :, 0],
        windows[:, :, :, 1],
        preferred_element_type=jnp.float32,
    ) / math.sqrt(HDIM)
    visible = (regions[:, :, None] == regions[:, None, :])[None, :, None]
    scores = jnp.where(visible, scores, -1e30)
    highest = jnp.max(scores, axis=-1, keepdims=True)
    expo_terms = jnp.where(visible, jnp.exp(scores - highest), 0.0)
    weights = (expo_terms / jnp.sum(expo_terms, axis=-1, keepdims=True)).astype(jnp.bfloat16)
    return jnp.einsum(
        "bwhqk,bwkhd->bwqhd", weights, windows[:, :, :, 2], preferred_element_type=jnp.float32
    ).astype(jnp.bfloat16)


def local_tiles(store, sample_index, region_ids, w_embed, attn_gain, w_qkv, w_out, out_gain, w_dec):
    lon_count = lax.axis_size("lon")
    slots_here, rows_here, width_all, patch_len = store.shape
    patch_cols = width_all // lon_count
    patch_rows = rows_here * lon_count
    half_win = WIN // 2
    ext_rows = patch_rows + WIN
    ext_cols = patch_cols + WIN
    own_slots = lax.axis_index("buf") * slots_here + jnp.arange(slots_here, dtype=jnp.int32)
    matches = own_slots[:, None] == sample_index[None, :]
    occupied = jnp.any(matches, axis=1)
    local_rows = store.reshape(slots_here, 1, rows_here, lon_count, patch_cols, patch_len)
    tile_data = lax.all_to_all(local_rows, "lon", split_axis=3, concat_axis=1, tiled=True)
    patches = tile_data.reshape(-1, patch_len)
    embedded = jnp.dot(patches, w_embed, preferred_element_type=jnp.float32).astype(jnp.bfloat16)
    normed = layer_norm(embedded.astype(jnp.float32), attn_gain).astype(jnp.bfloat16)
    normed = normed.reshape(slots_here, patch_rows, patch_cols, D)
    widened = with_halo(normed, (("lat", 1), ("lon", 2)), half_win)
    projected = jnp.dot(widened.reshape(-1, D), w_qkv, preferred_element_type=jnp.float32).astype(
        jnp.bfloat16
    )
    windows = projected.reshape(
        slots_here, ext_rows // WIN, WIN, ext_cols // WIN, WIN, 3, HEADS, HDIM
    )
    windows = windows.transpose(0, 1, 3, 2, 4, 5, 6, 7).reshape(
        slots_here, -1, WIN * WIN, 3, HEADS, HDIM
    )
    total_rows, total_cols = region_ids.shape
    row_pick = (
        lax.axis_index("lat") * patch_rows - half_win + jnp.arange(ext_rows, dtype=jnp.int32)
    ) % total_rows
    col_pick = (
        lax.axis_index("lon") * patch_cols - half_win + jnp.arange(ext_cols, dtype=jnp.int32)
    ) % total_cols
    local_regions = jnp.take(jnp.take(region_ids, row_pick, axis=0), col_pick, axis=1)
    region_windows = (
        local_regions.reshape(ext_rows // WIN, WIN, ext_cols // WIN, WIN)
        .transpose(0, 2, 1, 3)
        .reshape(-1, WIN * WIN)
    )
    mixed_heads = window_mix(windows, region_windows)
    placed = mixed_heads.reshape(slots_here, ext_rows // WIN, ext_cols // WIN, WIN, WIN, D)
    placed = placed.transpose(0, 1, 3, 2, 4, 5).reshape(slots_here, ext_rows, ext_cols, D)
    placed = placed[:, half_win : half_win + patch_rows, half_win : half_win + patch_cols].reshape(
        -1, D
    )
    updated = embedded.astype(jnp.float32) + jnp.dot(
        placed, w_out, preferred_element_type=jnp.float32
    )
    final_norm = layer_norm(updated, out_gain).astype(jnp.bfloat16)
    predicted = (
        patches.astype(jnp.float32) + jnp.dot(final_norm, w_dec, preferred_element_type=jnp.float32)
    ).astype(jnp.bfloat16)
    outgoing = predicted.reshape(slots_here, lon_count, rows_here, 1, patch_cols, patch_len)
    returned = lax.all_to_all(outgoing, "lon", split_axis=1, concat_axis=3, tiled=True)
    strip_data = returned.reshape(slots_here, rows_here, width_all, patch_len)
    return jnp.where(occupied[:, None, None, None], strip_data, store)


def to_windows(values):
    rows, cols = HALF, values.shape[0] // HALF
    parts = [pltpu.roll(values[cols * i : cols * (i + 1)], cols - HALF, 0) for i in range(rows)]
    return jnp.concatenate(
        [parts[i][WIN * c : WIN * (c + 1)] for c in range(cols // WIN) for i in range(rows)], axis=0
    )


def from_windows(values):
    rows, cols = HALF, values.shape[0] // HALF
    parts = []
    for i in range(rows):
        line = jnp.concatenate(
            [
                values[WIN * (rows * c + i) : WIN * (rows * c + i + 1)]
                for c in range(cols // WIN)
            ],
            axis=0,
        )
        parts.append(pltpu.roll(line, HALF, 0))
    return jnp.concatenate(parts, axis=0)


def embed_slot(patches, w_embed, gain):
    embedded = jnp.dot(patches, w_embed, preferred_element_type=jnp.float32).astype(jnp.bfloat16)
    embedded = to_windows(embedded.astype(jnp.float32))
    normed = layer_norm(embedded, gain).astype(jnp.bfloat16)
    return embedded.astype(jnp.bfloat16), normed


NT = (((1,), (1,)), ((), ()))
TN = (((0,), (0,)), ((), ()))
GROUP = 4
WIDE = GROUP * HDIM
PER = WIN * HALF


def attend_slot(query, kv_own, kv_other, q_regions, k_regions):
    shape = (GROUP * PER, WIDE)
    pick = (
        lax.broadcasted_iota(jnp.int32, shape, 0) // PER
        == lax.broadcasted_iota(jnp.int32, shape, 1) // HDIM
    )
    head_mask = jnp.where(pick, 1.0, 0.0).astype(jnp.bfloat16)
    windows = query.shape[0] // PER
    kvs, scores, weights, mixed = [], [], [], []
    for c in range(windows):
        at = slice(PER * c, PER * (c + 1))
        kvs.append(jnp.concatenate([kv_own[at], kv_other[at]], axis=0))
        for g in range(HEADS // GROUP):
            cols = slice(WIDE * g, WIDE * (g + 1))
            queries = jnp.concatenate([query[at, cols]] * GROUP, axis=0) * head_mask
            scores.append(
                lax.dot_general(kvs[c][:, cols], queries, NT, preferred_element_type=jnp.float32)
            )
    for c in range(windows):
        seen = k_regions[:, c : c + 1] == q_regions[c : c + 1, :]
        for g in range(HEADS // GROUP):
            part = jnp.where(seen, scores[2 * c + g], -1e30)
            expo = jnp.exp(part - jnp.max(part, axis=0, keepdims=True))
            total = jnp.sum(expo, axis=0, keepdims=True)
            weights.append((expo * (1.0 / total)).astype(jnp.bfloat16))
    for c in range(windows):
        groups = []
        for g in range(HEADS // GROUP):
            heads = lax.dot_general(
                weights[2 * c + g],
                kvs[c][:, D + WIDE * g : D + WIDE * (g + 1)],
                TN,
                preferred_element_type=jnp.float32,
            )
            heads = jnp.where(pick, heads, 0.0)
            total = heads[:PER]
            for h in range(1, GROUP):
                total = total + heads[PER * h : PER * (h + 1)]
            groups.append(total)
        mixed.append(jnp.concatenate(groups, axis=1).astype(jnp.bfloat16))
    return jnp.concatenate(mixed, axis=0)


def region_tables(own, far):
    rows, cols = own.shape
    windows = cols // WIN
    lines = [own[i : i + 1] for i in range(rows)] + [far[i : i + 1] for i in range(rows)]
    wide = jnp.concatenate([jnp.broadcast_to(line, (WIN, cols)) for line in lines], axis=0)
    row = lax.broadcasted_iota(jnp.int32, wide.shape, 0)
    col = lax.broadcasted_iota(jnp.int32, wide.shape, 1)
    kept = jnp.where((col + WIN - HALF) % WIN == row % WIN, wide, 0.0).astype(jnp.bfloat16)
    place = (lax.broadcasted_iota(jnp.int32, (windows, cols), 1) + cols - HALF) % cols // WIN
    here = place == lax.broadcasted_iota(jnp.int32, (windows, cols), 0)
    here = jnp.where(here, 1.0, 0.0).astype(jnp.bfloat16)
    k_regions = lax.dot_general(kept, here, NT, preferred_element_type=jnp.float32)
    q_rows = jnp.concatenate([kept[:PER]] * GROUP, axis=0)
    q_regions = lax.dot_general(here, q_rows, NT, preferred_element_type=jnp.float32)
    return q_regions, k_regions


def finish_part(embedded, mixed, w_out, gain):
    updated = embedded.astype(jnp.float32) + jnp.dot(
        mixed, w_out, preferred_element_type=jnp.float32
    )
    return layer_norm(updated, gain)


def decode_slot(patches, final, w_dec_t):
    return (
        patches.astype(jnp.float32)
        + lax.dot_general(
            final, w_dec_t, (((1,), (1,)), ((), ())), preferred_element_type=jnp.float32
        )
    ).astype(jnp.bfloat16)


def fused_kernel(
    sample_ref,
    region_ref,
    a_gain_ref,
    o_gain_ref,
    store_ref,
    w_embed_ref,
    w_qkv_ref,
    w_out_ref,
    w_dec_ref,
    new_ref,
    patches,
    w_embed,
    w_qkv,
    w_out,
    w_dec,
    embedded,
    own,
    far,
    own_qkv,
    finals,
    slot_sems,
    weight_sems,
    send_sems,
    recv_sems,
):
    slots, rows_here, cols, patch_len = store_ref.shape
    lon_count = lax.axis_size("lon")
    strips = lax.axis_size("lat") * lon_count
    mine = lax.axis_index("lat") * lon_count + lax.axis_index("lon")
    other = lax.rem(mine + 2 * lax.rem(mine, 2) - 1 + strips, strips)
    partner = {"lat": lax.div(other, lon_count), "lon": lax.rem(other, lon_count)}

    def slot_in(s):
        return pltpu.make_async_copy(store_ref.at[s], patches.at[s], slot_sems.at[s])

    tokens = rows_here * cols
    half = tokens // 2
    halves = [pl.ds(half * h, half) for h in range(2)]

    def send(k, h):
        return pltpu.make_async_remote_copy(
            src_ref=own.at[k, halves[h]],
            dst_ref=far.at[k, halves[h]],
            send_sem=send_sems.at[k, h],
            recv_sem=recv_sems.at[k, h],
            device_id=partner,
            device_id_type=pl.DeviceIdType.MESH,
        )

    weights = [
        pltpu.make_async_copy(src, dst, weight_sems.at[i])
        for i, (src, dst) in enumerate(
            ((w_embed_ref, w_embed), (w_qkv_ref, w_qkv), (w_out_ref, w_out), (w_dec_ref, w_dec))
        )
    ]
    weights[0].start()
    slot_in(0).start()

    barrier = pltpu.get_barrier_semaphore()
    pl.semaphore_signal(
        barrier, inc=1, device_id=partner, device_id_type=pl.DeviceIdType.MESH
    )
    q_regions, k_regions = region_tables(
        region_ref[pl.ds(mine * HALF, HALF), :].astype(jnp.float32),
        region_ref[pl.ds(other * HALF, HALF), :].astype(jnp.float32),
    )
    pl.semaphore_wait(barrier, 1)
    weights[0].wait()
    slot_in(0).wait()
    for s in range(1, slots):
        slot_in(s).start()
    for copy in weights[1:]:
        copy.start()

    @pl.loop(0, slots)
    def _(k):
        @pl.when(k > 0)
        def _():
            slot_in(k).wait()

        flat = patches[k].reshape(tokens, patch_len)
        embedded[k], own[k] = embed_slot(flat, w_embed[...], a_gain_ref[...])
        for h in range(2):
            send(k, h).start()

    weights[1].wait()

    @pl.loop(0, slots)
    def _(k):
        query = jnp.dot(own[k], w_qkv[:, :D], preferred_element_type=jnp.float32)
        own_qkv[k, :, :D] = (query * (1.0 / math.sqrt(HDIM))).astype(jnp.bfloat16)
        own_qkv[k, :, D:] = jnp.dot(
            own[k], w_qkv[:, D:], preferred_element_type=jnp.float32
        ).astype(jnp.bfloat16)

    weights[2].wait()
    weights[3].wait()
    windows = tokens // PER

    @pl.loop(0, slots)
    def _(k):
        for h in range(2):
            send(k, h).wait()
            at = slice(half * h, half * (h + 1))
            here = slice(windows // 2 * h, windows // 2 * (h + 1))
            kv_other = jnp.dot(far[k, at], w_qkv[:, D:], preferred_element_type=jnp.float32)
            mixed = attend_slot(
                own_qkv[k, at, :D],
                own_qkv[k, at, D:],
                kv_other.astype(jnp.bfloat16),
                q_regions[here],
                k_regions[:, here],
            )
            finals[at] = finish_part(embedded[k, at], mixed, w_out[...], o_gain_ref[...])
        final = from_windows(finals[...]).astype(jnp.bfloat16)
        slot = lax.axis_index("buf") * slots + k
        taken = sample_ref[0] == slot
        for b in range(1, sample_ref.shape[0]):
            taken = jnp.logical_or(taken, sample_ref[b] == slot)
        final = jnp.where(taken, final, jnp.zeros_like(final))
        flat = patches[k].reshape(tokens, patch_len)
        new_ref[k] = decode_slot(flat, final, w_dec[...]).reshape(rows_here, cols, patch_len)


def place_kernel(result_ref, new_ref, sems):
    slots, rows = new_ref.shape[:2]
    copies = [
        pltpu.make_async_copy(result_ref.at[s, i], new_ref.at[s, i], sems.at[s, i])
        for s in range(slots)
        for i in range(rows)
    ]
    for copy in copies:
        copy.start()
    for copy in copies:
        copy.wait()


def local_strips(
    store, sample_index, region_ids, w_embed, attn_gain, w_qkv, w_out, out_gain, w_dec
):
    slots, rows_here, cols, patch_len = store.shape
    tokens = rows_here * cols
    held = lambda *shape: pltpu.VMEM(shape, jnp.bfloat16)
    vmem = pl.BlockSpec(memory_space=pltpu.VMEM)
    hbm = pl.BlockSpec(memory_space=pl.ANY)
    result = pl.pallas_call(
        fused_kernel,
        in_specs=[pl.BlockSpec(memory_space=pltpu.SMEM), vmem, vmem, vmem] + [hbm] * 5,
        out_specs=vmem,
        out_shape=pltpu.VMEM(store.shape, store.dtype),
        scratch_shapes=[
            held(*store.shape),
            held(*w_embed.shape),
            held(*w_qkv.shape),
            held(*w_out.shape),
            held(*w_dec.shape[::-1]),
            held(slots, tokens, D),
            held(slots, tokens, D),
            held(slots, tokens, D),
            held(slots, tokens, 3 * D),
            pltpu.VMEM((tokens, D), jnp.float32),
            pltpu.SemaphoreType.DMA((slots,)),
            pltpu.SemaphoreType.DMA((4,)),
            pltpu.SemaphoreType.DMA((slots, 2)),
            pltpu.SemaphoreType.DMA((slots, 2)),
        ],
        compiler_params=pltpu.CompilerParams(
            vmem_limit_bytes=VMEM_LIMIT, collective_id=0, has_side_effects=True
        ),
    )(
        sample_index,
        region_ids,
        attn_gain[None],
        out_gain[None],
        store,
        w_embed,
        w_qkv,
        w_out,
        w_dec.T,
    )
    return pl.pallas_call(
        place_kernel,
        in_specs=[hbm],
        out_specs=hbm,
        out_shape=jax.ShapeDtypeStruct(store.shape, store.dtype),
        scratch_shapes=[pltpu.SemaphoreType.DMA((slots, rows_here))],
        compiler_params=pltpu.CompilerParams(vmem_limit_bytes=PICK_LIMIT),
    )(result)


def local(store, *rest):
    return (local_strips if store.shape[1] == HALF else local_tiles)(store, *rest)


def solution(mesh):
    return jax.shard_map(
        local,
        mesh=mesh,
        in_specs=(P("buf", ("lat", "lon"), None, None), P(), P(), P(), P(), P(), P(), P(), P()),
        out_specs=P("buf", ("lat", "lon"), None, None),
        check_vma=False,
    )
```
